128 devices in a mesh: req: 16 (over y, z_lo, core), ctx: 8 (over z_hi, x).
Axes of the slice: x: 4, y: 4, z: 4 (z_hi: 2, z_lo: 2; z = z_hi * 2 + z_lo), core: 2. Of those that a mesh axis runs over, the one named last changes fastest.
Arguments:
- queries: bfloat16 [16, 1024, 64, 128], P('req', 'ctx'), may hold values from -6 to 6
- span_keys: bfloat16 [16, 1024, 4, 128], P('req', 'ctx'), may hold values from -6 to 6
- span_values: bfloat16 [16, 1024, 4, 128], P('req', 'ctx'), may hold values from -6 to 6
- store_keys: bfloat16 [8, 512, 32, 4, 128], P('ctx', 'req'), may hold values from -6 to 6
- store_values: bfloat16 [8, 512, 32, 4, 128], P('ctx', 'req'), may hold values from -6 to 6
- page_home: int32 [8, 512], P('ctx'), may hold values from 0 to 511, as said below
- hits: int32 [16, 128], replicated, may hold values from 0 to 511, as said below
- counts: int32 [16], replicated, may hold values from 1 to 128, as said below
Outputs:
- attended: bfloat16 [16, 1024, 64, 128], P('req', 'ctx')
The draws below stay inside these ranges and needn't reach their ends.
Inputs may be any that keep to these rules, and one draw needn't show every extreme that they name: page_home[c] is a permutation of the storage rows 0 to 511 for each cycle slot c; storage row s of slot c lies on the store device of req index s // 32 and ctx index c. `hits`: entries j >= counts[r] are padding; for each request and each cycle slot c, of the 16 entries j with j mod 8 = c (padding included) exactly 1 lie on each req index of the store. `counts`: some request has exactly 128 cached pages.
All inputs are finite; a program needn't handle non-finite values.
Results may differ from the reference program's by a relative error of at most 0.0065.
Values may be sent and summed in bfloat16 or wider, within the bound.
A program may use at most 384 MiB of HBM per device.

```python
import jax
import jax.numpy as jnp
from jax import lax

HEADS = 64
KVH = 4
HD = 128
PAGE = 32
PER_SRC = 1
STORE_DEV = 32
GROUP = 16
REQS = 16
SPAN = 1024
PAGE_DEV = 16
MAX_PAGES = 128
STORE_PAGES = 512
N_CTX = 8


def page_layout(key):
    n_ctx = MAX_PAGES // PAGE_DEV
    keys = jax.random.split(jax.random.fold_in(key, 11), n_ctx)
    homes = jax.vmap(lambda k: jax.random.permutation(k, STORE_PAGES))(keys)
    return homes.astype(jnp.int32)


def draw_queries(key, part):
    key = jax.random.fold_in(key, 1)
    shape = (REQS, SPAN, HEADS, HD)
    base = jnp.clip(2.0 * jax.random.normal(key, shape, jnp.float32), -6.0, 6.0)
    return base.astype(jnp.bfloat16)


def draw_span_keys(key, part):
    key = jax.random.fold_in(key, 2)
    shape = (REQS, SPAN, KVH, HD)
    base = jnp.clip(jax.random.normal(key, shape, jnp.float32), -6.0, 6.0)
    return base.astype(jnp.bfloat16)


def draw_page_home(key, part):
    return page_layout(key)


def draw_hits(key, part):
    homes = page_layout(key)
    key = jax.random.fold_in(key, 5)
    n_ctx = MAX_PAGES // PAGE_DEV
    inverse = jnp.argsort(homes, axis=1, stable=True).astype(jnp.int32)
    group_keys = jax.random.split(jax.random.fold_in(key, 1), REQS * n_ctx)
    groups = jax.vmap(lambda k: jax.random.permutation(k, PAGE_DEV))(group_keys) // PER_SRC
    groups = groups.reshape(REQS, n_ctx, PAGE_DEV).astype(jnp.int32)
    slots = jax.random.randint(jax.random.fold_in(key, 2), (REQS, n_ctx, PAGE_DEV), 0, STORE_DEV, jnp.int32)
    rows = groups * STORE_DEV + slots
    column = jnp.arange(n_ctx, dtype=jnp.int32)[None, :, None]
    ids = inverse[column, rows]
    return jnp.transpose(ids, (0, 2, 1)).reshape(REQS, MAX_PAGES).astype(jnp.int32)


def draw_counts(key, part):
    key = jax.random.fold_in(key, 7)
    counts = jax.random.randint(jax.random.fold_in(key, 1), (REQS,), 1, MAX_PAGES + 1, jnp.int32)
    heavy = jax.random.randint(jax.random.fold_in(key, 2), (), 0, REQS, jnp.int32)
    return jnp.where(jnp.arange(REQS, dtype=jnp.int32) == heavy, MAX_PAGES, counts).astype(jnp.int32)


def steps_of(key, extent, cuts, smallest, largest):
    level, own = 1.0, jax.random.fold_in(key, 6)
    for dim, parts in cuts:
        steps = jnp.exp(jax.random.uniform(jax.random.fold_in(own, dim), (parts,), jnp.float32, smallest / len(cuts), largest / len(cuts)))
        level = level * jnp.repeat(steps, extent[dim] // parts).reshape([-1 if axis == dim else 1 for axis in range(len(extent))])
    return level


def gaussian(own_key, dims, width, bound, cuts=(), kind=jnp.bfloat16):
    drawn = width * jax.random.normal(own_key, dims, jnp.float32)
    if cuts:
        drawn = drawn * steps_of(own_key, dims, cuts, -0.22, 0.18)
    return jnp.clip(drawn, -bound, bound).astype(kind)


def setup_inputs(seed: int = 0) -> dict:
    key_of = jax.random.split(jax.random.key(seed), 9)
    return {
        "queries": draw_queries(jax.random.fold_in(key_of[8], 71), 0),
        "span_keys": draw_span_keys(jax.random.fold_in(key_of[8], 71), 0),
        "span_values": gaussian(key_of[2], (REQS, SPAN, KVH, HD), 1.0, 6.0, ((0, 16), (1, 8))),
        "store_keys": gaussian(key_of[3], (N_CTX, STORE_PAGES, PAGE, KVH, HD), 1.0, 6.0, ((0, 8), (1, 16))),
        "store_values": gaussian(key_of[4], (N_CTX, STORE_PAGES, PAGE, KVH, HD), 1.0, 6.0, ((0, 8), (1, 16))),
        "page_home": draw_page_home(jax.random.fold_in(key_of[8], 71), 0),
        "hits": draw_hits(jax.random.fold_in(key_of[8], 71), 0),
        "counts": draw_counts(jax.random.fold_in(key_of[8], 71), 0),
    }


def one_request(store_keys, store_values, page_home, inputs):
    query, new_keys, new_values, hit_row, count = inputs
    n_ctx = MAX_PAGES // PAGE_DEV
    page_index = jnp.arange(MAX_PAGES, dtype=jnp.int32)
    column = page_index % n_ctx
    rows = page_home[column, hit_row]
    pref_keys = store_keys[column, rows].reshape(MAX_PAGES * PAGE, KVH, HD)
    pref_values = store_values[column, rows].reshape(MAX_PAGES * PAGE, KVH, HD)
    keys = jnp.concatenate([pref_keys, new_keys], axis=0).astype(jnp.float32)
    values = jnp.concatenate([pref_values, new_values], axis=0).astype(jnp.float32)
    live = jnp.repeat(page_index < count, PAGE)
    token = jnp.arange(SPAN, dtype=jnp.int32)
    causal = token[None, :] <= token[:, None]
    visible = jnp.concatenate([jnp.broadcast_to(live[None, :], (SPAN, MAX_PAGES * PAGE)), causal], axis=1)
    query_groups = query.astype(jnp.float32).reshape(SPAN, KVH, GROUP, HD)
    scale = HD ** -0.5

    def one_head(kvh_index):
        qpart = lax.dynamic_index_in_dim(query_groups, kvh_index, 1, keepdims=False)
        kpart = lax.dynamic_index_in_dim(keys, kvh_index, 1, keepdims=False)
        vpart = lax.dynamic_index_in_dim(values, kvh_index, 1, keepdims=False)
        scores = jnp.einsum("tgd,sd->tgs", qpart, kpart, precision=lax.Precision.HIGHEST) * scale
        scores = jnp.where(visible[:, None, :], scores, -jnp.inf)
        peak = jnp.max(scores, axis=-1, keepdims=True)
        weights = jnp.exp(scores - peak)
        total = jnp.sum(weights, axis=-1)
        rounded = lax.optimization_barrier(weights.astype(jnp.bfloat16)).astype(jnp.float32)
        summed = jnp.einsum("tgs,sd->tgd", rounded, vpart, precision=lax.Precision.HIGHEST)
        return summed / total[..., None]

    heads_out = lax.map(one_head, jnp.arange(KVH, dtype=jnp.int32))
    return jnp.transpose(heads_out, (1, 0, 2, 3)).reshape(SPAN, HEADS, HD).astype(jnp.bfloat16)


def partial_request(store_keys, store_values, page_home):
    def apply_one(inputs):
        return one_request(store_keys, store_values, page_home, inputs)
    return apply_one


def reference(queries, span_keys, span_values, store_keys, store_values, page_home, hits, counts):
    return lax.map(partial_request(store_keys, store_values, page_home), (queries, span_keys, span_values, hits, counts))
```

```python
import functools

import jax
import jax.numpy as jnp
from jax import lax
from jax.experimental import pallas as pl
from jax.experimental.pallas import tpu as pltpu
from jax.sharding import PartitionSpec as P

MESH = pl.DeviceIdType.MESH
F32 = jnp.float32
BF16 = jnp.bfloat16
NT = (((1,), (1,)), ((), ()))
NN = (((1,), (0,)), ((), ()))
DEAD = 448.0
LOG2E = 1.4426950408889634
ROWS = 256
CHUNK = 1024


def pack_kernel(
    dims, hits, counts, home, sk_hbm, sv_hbm, stk_hbm, stv_hbm, send, span_send,
    slots, lives, store, span_in, local_sem,
):
    n_req, n_ctx, heads, store_dev, page_len, tokens, group, hd = dims
    piece = page_len * heads
    me_req = lax.axis_index("req")
    me_ctx = lax.axis_index("ctx")

    load_k = pltpu.make_async_copy(stk_hbm, store.at[0], local_sem.at[0])
    load_v = pltpu.make_async_copy(stv_hbm, store.at[1], local_sem.at[1])
    load_sk = pltpu.make_async_copy(sk_hbm, span_in.at[0], local_sem.at[2])
    load_sv = pltpu.make_async_copy(sv_hbm, span_in.at[1], local_sem.at[3])
    load_sk.start()
    load_sv.start()
    load_k.start()
    load_v.start()

    def find(r, _):
        slot = jnp.int32(0)
        live = jnp.int32(0)
        for i in range(n_req):
            j = i * n_ctx + me_ctx
            row = home[0, hits[r, j]]
            mine = lax.div(row, store_dev) == me_req
            slot = jnp.where(mine, lax.rem(row, store_dev), slot)
            live = jnp.where(mine, (j < counts[r]).astype(jnp.int32), live)
        slots[r] = slot
        lives[r] = live
        return 0

    lax.fori_loop(0, n_req, find, 0)

    to = lax.broadcasted_iota(jnp.int32, (piece, piece), 0)
    frm = lax.broadcasted_iota(jnp.int32, (piece, piece), 1)
    swap = (lax.rem(to, page_len) * heads + lax.div(to, page_len) == frm).astype(F32).astype(BF16)

    load_sk.wait()
    load_sv.wait()
    for g in range(tokens // page_len):
        pair = jnp.concatenate(
            [span_in[0, g * piece : (g + 1) * piece, :], span_in[1, g * piece : (g + 1) * piece, :]], axis=1
        )
        moved = lax.dot_general(swap, pair, NN, preferred_element_type=F32).astype(BF16)
        for h in range(heads):
            span_send[h, g * page_len : (g + 1) * page_len, :] = moved[h * page_len : (h + 1) * page_len, :]
    load_k.wait()
    load_v.wait()

    def pack(r, _):
        at = pl.ds(pl.multiple_of(slots[r] * piece, piece), piece)
        live = lives[r] > 0
        pair = jnp.concatenate([store[0, at, :], store[1, at, :]], axis=1)
        moved = lax.dot_general(swap, pair, NN, preferred_element_type=F32)
        lane = lax.broadcasted_iota(jnp.int32, (1, 2 * hd), 1)
        filler = jnp.where(lane < hd, DEAD, 0.0)
        moved = jnp.where(live, moved, jnp.broadcast_to(filler, moved.shape)).astype(BF16)
        for h in range(heads):
            send[r, h] = moved[h * page_len : (h + 1) * page_len, :]
        return 0

    lax.fori_loop(0, n_req, pack, 0)


def kernel(
    dims, q_hbm, send, span_send, out_hbm, qbuf, kv, acc, peak, ostage,
    own_sem, page_send, page_recv, span_sent, span_recv, q_sent, q_recv, o_sent, o_recv,
):
    n_req, n_ctx, heads, store_dev, page_len, tokens, group, hd = dims
    rows = tokens * group
    prefix = n_req * n_ctx * page_len
    me_req = lax.axis_index("req")
    me_ctx = lax.axis_index("ctx")
    col = lax.rem(me_ctx, heads)
    half = lax.div(me_ctx, heads)
    scale = hd ** -0.5 * LOG2E

    barrier = pltpu.get_barrier_semaphore()
    n_dev = n_req * n_ctx

    def greet(o, _):
        req = lax.rem(me_req + lax.div(o, n_ctx), n_req)
        ctx = lax.rem(me_ctx + lax.rem(o, n_ctx), n_ctx)
        pl.semaphore_signal(barrier, inc=1, device_id=(req, ctx), device_id_type=MESH)
        return 0

    lax.fori_loop(1, n_dev, greet, 0)
    pl.semaphore_wait(barrier, n_dev - 1)

    span_at = pl.ds(pl.multiple_of(prefix + me_ctx * tokens, tokens), tokens)
    span_dst = kv.at[span_at, pl.ds(0, 2 * hd)]
    pltpu.make_async_copy(span_send.at[col], span_dst, span_recv).start()

    def send_span(o, _):
        ctx = lax.rem(me_ctx + o, n_ctx)
        pltpu.make_async_remote_copy(
            span_send.at[lax.rem(ctx, heads)], span_dst, span_sent, span_recv,
            device_id=(me_req, ctx), device_id_type=MESH,
        ).start()
        return 0

    lax.fori_loop(1, n_ctx, send_span, 0)
    page_at = pl.ds(pl.multiple_of((me_ctx * n_req + me_req) * page_len, page_len), page_len)
    page_dst = kv.at[page_at, pl.ds(0, 2 * hd)]
    pltpu.make_async_copy(send.at[me_req, col], page_dst, page_recv.at[me_ctx]).start()

    def send_page(o, _):
        dc = lax.div(o, n_req)
        req = lax.rem(me_req + lax.rem(o, n_req), n_req)
        ctx = lax.rem(me_ctx + dc, n_ctx)
        pltpu.make_async_remote_copy(
            send.at[req, lax.rem(ctx, heads)], page_dst, page_send, page_recv.at[me_ctx],
            device_id=(req, ctx), device_id_type=MESH,
        ).start()
        return 0

    def q_src(c):
        return q_hbm.at[:, pl.ds(pl.multiple_of(c * group, group), group), :]

    pltpu.make_async_copy(q_src(col), qbuf.at[0], q_recv.at[0]).start()
    lax.fori_loop(1, n_dev, send_page, 0)

    def send_q(o, _):
        to_col = lax.rem(col + o, heads)
        pltpu.make_async_remote_copy(
            q_src(to_col), qbuf.at[o], q_sent, q_recv.at[o],
            device_id=(me_req, half * heads + to_col), device_id_type=MESH,
        ).start()
        return 0

    lax.fori_loop(1, heads, send_q, 0)

    def whole(ref, sem):
        return pltpu.make_async_copy(ref, ref, sem)

    whole(kv.at[pl.ds(prefix, n_ctx * tokens), pl.ds(0, 2 * hd)], span_recv).wait()
    kv[prefix : prefix + n_ctx * tokens, 2 * hd :] = jnp.ones((n_ctx * tokens, hd), BF16)
    per_slot = n_req * page_len

    def settle(c):
        at = pl.ds(pl.multiple_of(c * per_slot, per_slot), per_slot)
        whole(kv.at[at, pl.ds(0, 2 * hd)], page_recv.at[c]).wait()
        key0 = kv[prefix : prefix + 16, 0:hd].astype(F32)[0:1, :]
        raw = kv[at, 0:hd].astype(F32)
        dead = raw > 100.0
        kv[at, 0:hd] = jnp.where(dead, key0, raw).astype(BF16)
        kv[at, 2 * hd :] = jnp.where(dead, 0.0, 1.0).astype(BF16)

    def attend(dx, start, size, first_token):
        at = pl.ds(start, size)
        tiles = rows // ROWS
        toks = ROWS // group

        def score(t):
            q = qbuf[dx, t * toks : (t + 1) * toks].reshape(ROWS, hd)
            return lax.dot_general(q, kv[at, 0:hd], NT, preferred_element_type=F32)

        following = score(0)
        for t in range(tiles):
            s = following * scale
            if t + 1 < tiles:
                following = score(t + 1)
            if first_token is not None:
                token = lax.broadcasted_iota(jnp.int32, (ROWS, size), 0) // group + (first_token + t * toks)
                key = lax.broadcasted_iota(jnp.int32, (ROWS, size), 1)
                s = jnp.where(key <= token, s, -1e30)
            r = slice(t * ROWS, (t + 1) * ROWS)
            before = peak[r, :]
            now = jnp.maximum(before, jnp.max(s, axis=1, keepdims=True))
            peak[r, :] = now
            factor = jnp.exp2(before - now)
            w = jnp.exp2(s - jnp.concatenate([now] * (size // hd), axis=1)).astype(BF16)
            wv = lax.dot_general(w, kv[at, hd:], NN, preferred_element_type=F32)
            acc[r, :] = acc[r, :] * jnp.concatenate([factor, factor], axis=1) + wv

    def block(dx, _):
        whole(qbuf.at[dx], q_recv.at[dx]).wait()
        acc[...] = jnp.zeros_like(acc)
        peak[...] = jnp.full(peak.shape, -1e30, F32)
        from_col = lax.rem(col - dx + heads, heads)
        first = (half * heads + from_col) * tokens

        slots_per = CHUNK // per_slot

        def chunk(i, _):
            c = lax.rem(lax.div(me_ctx, slots_per) + n_ctx // slots_per - i, n_ctx // slots_per)

            @pl.when(dx == 0)
            def _():
                for u in range(slots_per):
                    settle(c * slots_per + u)

            attend(dx, pl.multiple_of(c * CHUNK, CHUNK), CHUNK, None)
            return 0

        lax.fori_loop(0, prefix // CHUNK, chunk, 0)
        for z in range(n_ctx // heads):

            @pl.when(half == z)
            def _():
                attend(dx, prefix, (z + 1) * heads * tokens, first)

        out = acc[:, 0:hd] / acc[:, hd:]
        ostage[dx] = out.astype(BF16).reshape(tokens, group, hd)
        o_dst = out_hbm.at[:, pl.ds(pl.multiple_of(col * group, group), group), :]

        @pl.when(dx == 0)
        def _():
            pltpu.make_async_copy(ostage.at[dx], o_dst, own_sem).start()

        @pl.when(dx > 0)
        def _():
            pltpu.make_async_remote_copy(
                ostage.at[dx], o_dst, o_sent, o_recv,
                device_id=(me_req, half * heads + from_col), device_id_type=MESH,
            ).start()

        return 0

    lax.fori_loop(0, heads, block, 0)
    pltpu.make_async_copy(ostage.at[0], ostage.at[0], own_sem).wait()
    whole(kv.at[pl.ds(0, (n_ctx - 1) * tokens), pl.ds(0, 2 * hd)], span_sent).wait()
    whole(kv.at[pl.ds(0, (n_dev - 1) * page_len), pl.ds(0, 2 * hd)], page_send).wait()
    whole(qbuf.at[pl.ds(0, heads - 1)], q_sent).wait()
    whole(ostage.at[pl.ds(0, heads - 1)], o_sent).wait()
    whole(ostage.at[pl.ds(0, heads - 1)], o_recv).wait()


def per_device(queries, span_keys, span_values, store_keys, store_values, page_home, hits, counts):
    n_req = lax.axis_size("req")
    n_ctx = lax.axis_size("ctx")
    _, tokens, q_heads, hd = queries.shape
    heads = span_keys.shape[2]
    group = q_heads // heads
    _, store_dev, page_len, _, _ = store_keys.shape
    dims = (n_req, n_ctx, heads, store_dev, page_len, tokens, group, hd)
    rows = tokens * group
    keys = n_req * n_ctx * page_len + n_ctx * tokens
    smem = pl.BlockSpec(memory_space=pltpu.SMEM)
    hbm = pl.BlockSpec(memory_space=pl.ANY)
    dma = pltpu.SemaphoreType.DMA
    vmem = pl.BlockSpec(memory_space=pltpu.VMEM)
    send, span_send = pl.pallas_call(
        functools.partial(pack_kernel, dims),
        out_shape=(
            jax.ShapeDtypeStruct((n_req, heads, page_len, 2 * hd), BF16),
            jax.ShapeDtypeStruct((heads, tokens, 2 * hd), BF16),
        ),
        in_specs=[smem] * 3 + [hbm] * 4,
        out_specs=(vmem, vmem),
        scratch_shapes=[
            pltpu.SMEM((n_req,), jnp.int32),
            pltpu.SMEM((n_req,), jnp.int32),
            pltpu.VMEM((2, store_dev * page_len * heads, hd), BF16),
            pltpu.VMEM((2, tokens * heads, hd), BF16),
            dma((4,)),
        ],
        compiler_params=pltpu.CompilerParams(vmem_limit_bytes=32 * 2**20),
        name="pack_pages",
    )(
        hits, counts, page_home,
        span_keys.reshape(tokens * heads, hd),
        span_values.reshape(tokens * heads, hd),
        store_keys.reshape(store_dev * page_len * heads, hd),
        store_values.reshape(store_dev * page_len * heads, hd),
    )
    out = pl.pallas_call(
        functools.partial(kernel, dims),
        out_shape=jax.ShapeDtypeStruct((tokens, q_heads, hd), BF16),
        in_specs=[hbm] * 3,
        out_specs=hbm,
        scratch_shapes=[
            pltpu.VMEM((heads, tokens, group, hd), BF16),
            pltpu.VMEM((keys, 3 * hd), BF16),
            pltpu.VMEM((rows, 2 * hd), F32),
            pltpu.VMEM((rows, hd), F32),
            pltpu.VMEM((heads, tokens, group, hd), BF16),
            dma,
            dma,
            dma((n_ctx,)),
            dma,
            dma,
            dma,
            dma((heads,)),
            dma,
            dma,
        ],
        compiler_params=pltpu.CompilerParams(
            collective_id=0, has_side_effects=True, vmem_limit_bytes=60 * 2**20
        ),
        name="attend_pages",
    )(queries[0], send, span_send)
    return out[None]


def solution(mesh):
    placed = (
        P("req", "ctx", None, None),
        P("req", "ctx", None, None),
        P("req", "ctx", None, None),
        P("ctx", "req", None, None, None),
        P("ctx", "req", None, None, None),
        P("ctx", None),
        P(),
        P(),
    )
    return jax.shard_map(
        per_device,
        mesh=mesh,
        in_specs=placed,
        out_specs=P("req", "ctx", None, None),
        check_vma=False,
    )
```

```python
import functools

import jax
import jax.numpy as jnp
from jax import lax
from jax.experimental import pallas as pl
from jax.experimental.pallas import tpu as pltpu
from jax.sharding import PartitionSpec as P

MESH = pl.DeviceIdType.MESH
F32 = jnp.float32
BF16 = jnp.bfloat16
NT = (((1,), (1,)), ((), ()))
NN = (((1,), (0,)), ((), ()))
DEAD = 448.0
LOG2E = 1.4426950408889634
ROWS = 256


def kernel(
    dims, hits, counts, home, q_hbm, sk_hbm, sv_hbm, stk_hbm, stv_hbm, out_hbm,
    store, span_in, send, span_send, qbuf, raw, kv, acc, peak, ostage,
    load_sem, page_sent, page_recv, span_sent, span_recv, pass_sent, pass_recv,
    span_pass_sent, span_pass_recv, q_sent, q_recv, o_sent, o_recv, own_sem,
):
    n_req, n_ctx, heads, store_dev, page_len, tokens, group, hd = dims
    halves = n_ctx // heads
    part = tokens // 2
    piece = page_len * heads
    per_slot = n_req * page_len
    near = heads * per_slot
    prefix = halves * near
    span = heads * tokens
    me_req = lax.axis_index("req")
    me_ctx = lax.axis_index("ctx")
    col = lax.rem(me_ctx, heads)
    half = lax.div(me_ctx, heads)
    partner = (me_req, (1 - half) * heads + col)
    scale = hd ** -0.5 * LOG2E
    both = pl.ds(0, 2 * hd)

    loads = [
        pltpu.make_async_copy(src, dst, load_sem.at[i])
        for i, (src, dst) in enumerate(
            [(sk_hbm, span_in.at[0]), (sv_hbm, span_in.at[1]), (stk_hbm, store.at[0]), (stv_hbm, store.at[1])]
        )
    ]
    for load in loads:
        load.start()

    def whole(ref, sem):
        return pltpu.make_async_copy(ref, ref, sem)

    def q_src(c, h):
        return q_hbm.at[pl.ds(h * part, part), pl.ds(pl.multiple_of(c * group, group), group), :]

    for h in range(2):
        pltpu.make_async_copy(q_src(col, h), qbuf.at[h], q_recv.at[h]).start()

    barrier = pltpu.get_barrier_semaphore()

    def near_device(o):
        req = lax.rem(me_req + lax.div(o, heads), n_req)
        return req, half * heads + lax.rem(col + lax.rem(o, heads), heads)

    def greet(o, _):
        pl.semaphore_signal(barrier, inc=1, device_id=near_device(o), device_id_type=MESH)
        return 0

    lax.fori_loop(1, n_req * heads, greet, 0)
    pl.semaphore_signal(barrier, inc=1, device_id=partner, device_id_type=MESH)

    to = lax.broadcasted_iota(jnp.int32, (piece, piece), 0)
    frm = lax.broadcasted_iota(jnp.int32, (piece, piece), 1)
    swap = (lax.rem(to, page_len) * heads + lax.div(to, page_len) == frm).astype(F32).astype(BF16)

    for load in loads[:2]:
        load.wait()
    for g in range(tokens // page_len):
        pair = jnp.concatenate(
            [span_in[0, g * piece : (g + 1) * piece, :], span_in[1, g * piece : (g + 1) * piece, :]], axis=1
        )
        moved = lax.dot_general(swap, pair, NN, preferred_element_type=F32).astype(BF16)
        for h in range(heads):
            span_send[h, g * page_len : (g + 1) * page_len, :] = moved[h * page_len : (h + 1) * page_len, :]
    for load in loads[2:]:
        load.wait()

    def pack(r, _):
        slot = jnp.int32(0)
        live = jnp.int32(0)
        for i in range(n_req):
            j = i * n_ctx + me_ctx
            row = home[0, hits[r, j]]
            mine = (lax.div(row, store_dev) == me_req).astype(jnp.int32)
            slot = slot + mine * lax.rem(row, store_dev)
            live = live + mine * (j < counts[r]).astype(jnp.int32)
        live = live.astype(F32)
        pair = jnp.concatenate([store[0, slot], store[1, slot]], axis=1)
        moved = lax.dot_general(swap, pair, NN, preferred_element_type=F32)
        lane = lax.broadcasted_iota(jnp.int32, moved.shape, 1)
        filler = jnp.where(lane < hd, DEAD, 0.0)
        moved = (moved * live + filler * (1.0 - live)).astype(BF16)
        for h in range(heads):
            send[r, h] = moved[h * page_len : (h + 1) * page_len, :]
        return 0

    lax.fori_loop(0, n_req, pack, 0)
    pl.semaphore_wait(barrier, n_req * heads)

    span_dst = raw.at[pl.ds(pl.multiple_of(prefix + me_ctx * tokens, tokens), tokens), both]
    pltpu.make_async_copy(span_send.at[col], span_dst, span_recv).start()

    def send_span(o, _):
        c = lax.rem(col + o, heads)
        pltpu.make_async_remote_copy(
            span_send.at[c], span_dst, span_sent, span_recv,
            device_id=(me_req, half * heads + c), device_id_type=MESH,
        ).start()
        return 0

    lax.fori_loop(1, heads, send_span, 0)

    page_dst = raw.at[pl.ds(pl.multiple_of((me_ctx * n_req + me_req) * page_len, page_len), page_len), both]
    pltpu.make_async_copy(send.at[me_req, col], page_dst, page_recv.at[col]).start()

    def send_page(req, c):
        pltpu.make_async_remote_copy(
            send.at[req, c], page_dst, page_sent, page_recv.at[col],
            device_id=(req, half * heads + c), device_id_type=MESH,
        ).start()

    def send_same(o, _):
        send_page(lax.rem(me_req + o, n_req), col)
        return 0

    lax.fori_loop(1, n_req, send_same, 0)

    def send_sides(o, _):
        req = lax.rem(me_req + o, n_req)
        send_page(req, lax.rem(col + 1, heads))
        send_page(req, lax.rem(col + heads - 1, heads))
        return 0

    lax.fori_loop(0, n_req, send_sides, 0)

    def send_far(o, _):
        send_page(lax.rem(me_req + o, n_req), lax.rem(col + 2, heads))
        return 0

    lax.fori_loop(0, n_req, send_far, 0)

    def unit_of(i):
        far = lax.div(i, 4)
        slot = (1 - far) * (1 + 2 * lax.rem(i, 2)) + far * 2
        return slot, (1 - far) * lax.div(i, 2) + far * (i - 4)

    def send_q(i, _):
        slot, h = unit_of(i)
        c = lax.rem(col + slot, heads)
        u = slot * 2 + h
        pltpu.make_async_remote_copy(
            q_src(c, h), qbuf.at[u], q_sent, q_recv.at[u],
            device_id=(me_req, half * heads + c), device_id_type=MESH,
        ).start()
        return 0

    units = 2 * (heads - 1)
    lax.fori_loop(0, units, send_q, 0)

    def settle(start, size, key0):
        at = pl.ds(start, size)
        keys = raw[at, 0:hd].astype(F32)
        dead = keys > 100.0
        kv[at, 0:hd] = jnp.where(dead, key0, keys).astype(BF16)
        kv[at, hd : 2 * hd] = raw[at, hd : 2 * hd]
        kv[at, 2 * hd :] = jnp.where(dead, 0.0, 1.0).astype(BF16)

    part_rows = part * group
    tiles = part_rows // ROWS
    toks = ROWS // group

    def attend(u, count, segments, fresh, last, first_token):
        base = u * part_rows
        steps = [(t, g) for t in range(count * tiles) for g in range(len(segments))]

        def score(t, g):
            start, size, _ = segments[g]
            q = qbuf[u + t // tiles, (t % tiles) * toks : (t % tiles + 1) * toks].reshape(ROWS, hd)
            return lax.dot_general(q, kv[pl.ds(start, size), 0:hd], NT, preferred_element_type=F32)

        following = score(*steps[0])
        for n, (t, g) in enumerate(steps):
            s = following * scale
            if n + 1 < len(steps):
                following = score(*steps[n + 1])
            start, size, first_key = segments[g]
            at = pl.ds(pl.multiple_of(base + t * ROWS, ROWS), ROWS)
            if first_key is not None:
                token = lax.broadcasted_iota(jnp.int32, (ROWS, size), 0) // group + (first_token + t * toks - first_key)
                key = lax.broadcasted_iota(jnp.int32, (ROWS, size), 1)
                s = jnp.where(key <= token, s, -1e30)
            top = jnp.max(s, axis=1, keepdims=True)
            if g == 0 and fresh:
                now = jnp.broadcast_to(top, (ROWS, hd))
            else:
                before = peak[at, :] if g == 0 else now
                now = jnp.maximum(before, top)
                factor = jnp.exp2(before - now)
            w = jnp.exp2(s - jnp.concatenate([now] * (size // hd), axis=1)).astype(BF16)
            wv = lax.dot_general(w, kv[pl.ds(start, size), hd:], NN, preferred_element_type=F32)
            if g == 0 and fresh:
                total = wv
            else:
                total = (acc[at, :] if g == 0 else total) * jnp.concatenate([factor, factor], axis=1) + wv
            if g + 1 == len(segments):
                if last:
                    out = total[:, 0:hd] / total[:, hd:]
                    ostage[u + t // tiles, (t % tiles) * toks : (t % tiles + 1) * toks] = out.astype(BF16).reshape(
                        toks, group, hd
                    )
                else:
                    peak[at, :] = now
                    acc[at, :] = total

    span_at = pl.multiple_of(prefix + half * span, span)
    whole(raw.at[pl.ds(span_at, span), both], span_recv).wait()
    span_pass = pltpu.make_async_remote_copy(
        raw.at[pl.ds(prefix, span), both], raw.at[pl.ds(prefix, span), both], span_pass_sent, span_pass_recv,
        device_id=partner, device_id_type=MESH,
    )

    @pl.when(half == 0)
    def _():
        span_pass.start()

    key0 = raw[pl.ds(span_at, 16), 0:hd].astype(F32)[0:1, :]
    settle(span_at, span, key0)
    own_rows = slice(0, 2 * part_rows)
    acc[own_rows, :] = jnp.zeros((2 * part_rows, 2 * hd), F32)
    peak[own_rows, :] = jnp.full((2 * part_rows, hd), -1e30, F32)
    for h in range(2):
        whole(qbuf.at[h], q_recv.at[h]).wait()

    def chunk(i, _):
        c = lax.rem(col + (1 - lax.div(i, 3)) * i * (heads - 1) * (1 - lax.div(i, 2)) + lax.div(i, 2) * (i - 1), heads)
        start = pl.multiple_of((half * heads + c) * per_slot, per_slot)
        here = raw.at[pl.ds(start, per_slot), both]
        whole(here, page_recv.at[c]).wait()
        pltpu.make_async_remote_copy(
            here, here, pass_sent, pass_recv.at[c], device_id=partner, device_id_type=MESH
        ).start()
        settle(start, per_slot, key0)
        attend(0, 2, [(start, per_slot, None)], False, False, None)
        return 0

    lax.fori_loop(0, heads, chunk, 0)
    near_at = pl.multiple_of(half * near, near)
    far_at = pl.multiple_of((1 - half) * near, near)
    cut = near // 2

    def halves_of(at):
        return [(pl.multiple_of(at + i * cut, cut), cut, None) for i in range(2)]

    def first_pass(i, _):
        slot, h = unit_of(i)
        u = slot * 2 + h
        whole(qbuf.at[u], q_recv.at[u]).wait()
        attend(u, 1, halves_of(near_at), True, False, None)
        return 0

    lax.fori_loop(0, units, first_pass, 0)

    for c in range(heads):
        start = pl.multiple_of(far_at + c * per_slot, per_slot)
        whole(raw.at[pl.ds(start, per_slot), both], pass_recv.at[c]).wait()
        settle(start, per_slot, key0)

    @pl.when(half == 1)
    def _():
        span_pass.wait_recv()
        settle(prefix, span, key0)

    def second_pass(j, _):
        own = lax.div(j, units)
        slot, h = unit_of((1 - own) * (units - 1 - j))
        slot = (1 - own) * slot
        h = (1 - own) * h + own * (j - units)
        u = slot * 2 + h
        from_col = lax.rem(col - slot + heads, heads)
        first_token = from_col * tokens + h * part
        for z in range(halves):

            @pl.when(half == z)
            def _():
                spans = [(prefix + i * span, span, 0 if i == z else None) for i in range(z + 1)]
                attend(u, 1, halves_of(far_at) + spans, False, True, first_token)

        o_dst = out_hbm.at[pl.ds(pl.multiple_of(h * part, part), part), pl.ds(pl.multiple_of(col * group, group), group), :]

        @pl.when(own == 1)
        def _():
            pltpu.make_async_copy(ostage.at[u], o_dst, own_sem).start()

        @pl.when(own == 0)
        def _():
            pltpu.make_async_remote_copy(
                ostage.at[u], o_dst, o_sent, o_recv,
                device_id=(me_req, half * heads + from_col), device_id_type=MESH,
            ).start()

        return 0

    lax.fori_loop(0, 2 * heads, second_pass, 0)
    whole(ostage.at[pl.ds(0, 2)], own_sem).wait()
    whole(raw.at[pl.ds(0, (heads - 1) * tokens), both], span_sent).wait()
    whole(raw.at[pl.ds(0, (n_req * heads - 1) * page_len), both], page_sent).wait()
    whole(raw.at[pl.ds(0, near), both], pass_sent).wait()

    @pl.when(half == 0)
    def _():
        span_pass.wait_send()

    whole(qbuf.at[pl.ds(0, units)], q_sent).wait()
    whole(ostage.at[pl.ds(0, units)], o_sent).wait()
    whole(ostage.at[pl.ds(0, units)], o_recv).wait()


def per_device(queries, span_keys, span_values, store_keys, store_values, page_home, hits, counts):
    n_req = lax.axis_size("req")
    n_ctx = lax.axis_size("ctx")
    _, tokens, q_heads, hd = queries.shape
    heads = span_keys.shape[2]
    group = q_heads // heads
    _, store_dev, page_len, _, _ = store_keys.shape
    dims = (n_req, n_ctx, heads, store_dev, page_len, tokens, group, hd)
    rows = heads * tokens * group
    keys = n_req * n_ctx * page_len + n_ctx * tokens
    smem = pl.BlockSpec(memory_space=pltpu.SMEM)
    hbm = pl.BlockSpec(memory_space=pl.ANY)
    dma = pltpu.SemaphoreType.DMA
    out = pl.pallas_call(
        functools.partial(kernel, dims),
        out_shape=jax.ShapeDtypeStruct((tokens, q_heads, hd), BF16),
        in_specs=[smem] * 3 + [hbm] * 5,
        out_specs=hbm,
        scratch_shapes=[
            pltpu.VMEM((2, store_dev, page_len * heads, hd), BF16),
            pltpu.VMEM((2, tokens * heads, hd), BF16),
            pltpu.VMEM((n_req, heads, page_len, 2 * hd), BF16),
            pltpu.VMEM((heads, tokens, 2 * hd), BF16),
            pltpu.VMEM((2 * heads, tokens // 2, group, hd), BF16),
            pltpu.VMEM((keys, 2 * hd), BF16),
            pltpu.VMEM((keys, 3 * hd), BF16),
            pltpu.VMEM((rows, 2 * hd), F32),
            pltpu.VMEM((rows, hd), F32),
            pltpu.VMEM((2 * heads, tokens // 2, group, hd), BF16),
            dma((4,)),
            dma, dma((heads,)), dma, dma, dma, dma((heads,)), dma, dma, dma, dma((2 * heads,)), dma, dma, dma,
        ],
        compiler_params=pltpu.CompilerParams(
            collective_id=0, has_side_effects=True, vmem_limit_bytes=60 * 2**20
        ),
        name="attend_pages",
    )(
        hits, counts, page_home, queries[0],
        span_keys.reshape(tokens * heads, hd),
        span_values.reshape(tokens * heads, hd),
        store_keys.reshape(store_dev, page_len * heads, hd),
        store_values.reshape(store_dev, page_len * heads, hd),
    )
    return out[None]


def solution(mesh):
    placed = (
        P("req", "ctx", None, None),
        P("req", "ctx", None, None),
        P("req", "ctx", None, None),
        P("ctx", "req", None, None, None),
        P("ctx", "req", None, None, None),
        P("ctx", None),
        P(),
        P(),
    )
    return jax.shard_map(
        per_device,
        mesh=mesh,
        in_specs=placed,
        out_specs=P("req", "ctx", None, None),
        check_vma=False,
    )
```

```python
import functools

import jax
import jax.numpy as jnp
from jax import lax
from jax.experimental import pallas as pl
from jax.experimental.pallas import tpu as pltpu
from jax.sharding import PartitionSpec as P

MESH = pl.DeviceIdType.MESH
F32 = jnp.float32
BF16 = jnp.bfloat16
NT = (((1,), (1,)), ((), ()))
NN = (((1,), (0,)), ((), ()))
DEAD = 448.0
LOG2E = 1.4426950408889634
ROWS = 256


def kernel(
    dims, hits, counts, home, q_hbm, sk_hbm, sv_hbm, stk_hbm, stv_hbm, out_hbm,
    store, span_in, send, span_send, qbuf, raw, kv, acc, peak, ostage,
    load_sem, page_sent, page_recv, span_sent, span_recv, pass_sent, pass_recv,
    span_pass_sent, span_pass_recv, q_sent, q_recv, o_sent, o_recv, own_sem,
):
    n_req, n_ctx, heads, store_dev, page_len, tokens, group, hd = dims
    halves = n_ctx // heads
    part = tokens // 2
    piece = page_len * heads
    per_slot = n_req * page_len
    near = heads * per_slot
    prefix = halves * near
    span = heads * tokens
    me_req = lax.axis_index("req")
    me_ctx = lax.axis_index("ctx")
    col = lax.rem(me_ctx, heads)
    half = lax.div(me_ctx, heads)
    partner = (me_req, (1 - half) * heads + col)
    scale = hd ** -0.5 * LOG2E
    both = pl.ds(0, 2 * hd)

    loads = [
        pltpu.make_async_copy(src, dst, load_sem.at[i])
        for i, (src, dst) in enumerate(
            [(sk_hbm, span_in.at[0]), (sv_hbm, span_in.at[1]), (stk_hbm, store.at[0]), (stv_hbm, store.at[1])]
        )
    ]
    for load in loads:
        load.start()

    def whole(ref, sem):
        return pltpu.make_async_copy(ref, ref, sem)

    def q_src(c, h):
        return q_hbm.at[pl.ds(h * part, part), pl.ds(pl.multiple_of(c * group, group), group), :]

    for h in range(2):
        pltpu.make_async_copy(q_src(col, h), qbuf.at[h], q_recv.at[h]).start()

    barrier = pltpu.get_barrier_semaphore()

    def near_device(o):
        req = lax.rem(me_req + lax.div(o, heads), n_req)
        return req, half * heads + lax.rem(col + lax.rem(o, heads), heads)

    def greet(o, _):
        pl.semaphore_signal(barrier, inc=1, device_id=near_device(o), device_id_type=MESH)
        return 0

    lax.fori_loop(1, n_req * heads, greet, 0)
    pl.semaphore_signal(barrier, inc=1, device_id=partner, device_id_type=MESH)

    to = lax.broadcasted_iota(jnp.int32, (piece, piece), 0)
    frm = lax.broadcasted_iota(jnp.int32, (piece, piece), 1)
    swap = (lax.rem(to, page_len) * heads + lax.div(to, page_len) == frm).astype(F32).astype(BF16)

    for load in loads[:2]:
        load.wait()
    for g in range(tokens // page_len):
        pair = jnp.concatenate(
            [span_in[0, g * piece : (g + 1) * piece, :], span_in[1, g * piece : (g + 1) * piece, :]], axis=1
        )
        moved = lax.dot_general(swap, pair, NN, preferred_element_type=F32).astype(BF16)
        for h in range(heads):
            span_send[h, g * page_len : (g + 1) * page_len, :] = moved[h * page_len : (h + 1) * page_len, :]
    for load in loads[2:]:
        load.wait()

    first_row = me_req * store_dev
    group_of = 4

    def pack(r):
        slot = jnp.int32(0)
        live = jnp.int32(0)
        for i in range(n_req):
            j = i * n_ctx + me_ctx
            row = home[0, hits[r, j]] - first_row
            mine = jnp.logical_and(row >= 0, row < store_dev).astype(jnp.int32)
            slot = slot + mine * row
            live = live + mine * (j < counts[r]).astype(jnp.int32)
        live = live.astype(F32)
        pair = jnp.concatenate([store[0, slot], store[1, slot]], axis=1)
        moved = lax.dot_general(swap, pair, NN, preferred_element_type=F32)
        lane = lax.broadcasted_iota(jnp.int32, moved.shape, 1)
        filler = jnp.where(lane < hd, DEAD, 0.0)
        moved = (moved * live + filler * (1.0 - live)).astype(BF16)
        for h in range(heads):
            send[r, h] = moved[h * page_len : (h + 1) * page_len, :]

    def pack_group(i, _):
        for k in range(group_of):
            pack(i * group_of + k)
        return 0

    lax.fori_loop(0, n_req // group_of, pack_group, 0)
    pl.semaphore_wait(barrier, n_req * heads)

    span_dst = raw.at[pl.ds(pl.multiple_of(prefix + me_ctx * tokens, tokens), tokens), both]
    pltpu.make_async_copy(span_send.at[col], span_dst, span_recv).start()

    def send_span(o, _):
        c = lax.rem(col + o, heads)
        pltpu.make_async_remote_copy(
            span_send.at[c], span_dst, span_sent, span_recv,
            device_id=(me_req, half * heads + c), device_id_type=MESH,
        ).start()
        return 0

    lax.fori_loop(1, heads, send_span, 0)

    page_dst = raw.at[pl.ds(pl.multiple_of((me_ctx * n_req + me_req) * page_len, page_len), page_len), both]
    pltpu.make_async_copy(send.at[me_req, col], page_dst, page_recv.at[col]).start()

    def send_page(req, c):
        pltpu.make_async_remote_copy(
            send.at[req, c], page_dst, page_sent, page_recv.at[col],
            device_id=(req, half * heads + c), device_id_type=MESH,
        ).start()

    def mixed(o):
        return lax.rem(me_req + 5 * o, n_req)

    def send_same(o, _):
        send_page(mixed(o), col)
        return 0

    lax.fori_loop(1, n_req, send_same, 0)

    def send_sides(o, _):
        req = mixed(o)
        send_page(req, lax.rem(col + 1, heads))
        send_page(req, lax.rem(col + heads - 1, heads))
        return 0

    lax.fori_loop(0, n_req, send_sides, 0)

    def send_far(o, _):
        send_page(mixed(o), lax.rem(col + 2, heads))
        return 0

    lax.fori_loop(0, n_req, send_far, 0)

    def unit_of(i):
        far = lax.div(i, 4)
        slot = (1 - far) * (1 + 2 * lax.rem(i, 2)) + far * 2
        return slot, (1 - far) * lax.div(i, 2) + far * (i - 4)

    def send_q(i, _):
        slot, h = unit_of(i)
        c = lax.rem(col + slot, heads)
        u = slot * 2 + h
        pltpu.make_async_remote_copy(
            q_src(c, h), qbuf.at[u], q_sent, q_recv.at[u],
            device_id=(me_req, half * heads + c), device_id_type=MESH,
        ).start()
        return 0

    units = 2 * (heads - 1)
    lax.fori_loop(0, units, send_q, 0)

    def settle(start, size, key0):
        at = pl.ds(start, size)
        keys = raw[at, 0:hd].astype(F32)
        dead = keys > 100.0
        kv[at, 0:hd] = jnp.where(dead, key0, keys).astype(BF16)
        kv[at, hd : 2 * hd] = raw[at, hd : 2 * hd]
        kv[at, 2 * hd :] = jnp.where(dead, 0.0, 1.0).astype(BF16)

    part_rows = part * group
    tiles = part_rows // ROWS
    toks = ROWS // group

    def attend(u, count, segments, fresh, last, first_token):
        base = u * part_rows
        steps = [(t, g) for t in range(count * tiles) for g in range(len(segments))]

        def score(t, g):
            start, size, _ = segments[g]
            q = qbuf[u + t // tiles, (t % tiles) * toks : (t % tiles + 1) * toks].reshape(ROWS, hd)
            return lax.dot_general(q, kv[pl.ds(start, size), 0:hd], NT, preferred_element_type=F32)

        following = score(*steps[0])
        for n, (t, g) in enumerate(steps):
            s = following * scale
            if n + 1 < len(steps):
                following = score(*steps[n + 1])
            start, size, first_key = segments[g]
            at = pl.ds(pl.multiple_of(base + t * ROWS, ROWS), ROWS)
            if first_key is not None:
                token = lax.broadcasted_iota(jnp.int32, (ROWS, size), 0) // group + (first_token + t * toks - first_key)
                key = lax.broadcasted_iota(jnp.int32, (ROWS, size), 1)
                s = jnp.where(key <= token, s, -1e30)
            top = jnp.max(s, axis=1, keepdims=True)
            if g == 0 and fresh:
                now = jnp.broadcast_to(top, (ROWS, hd))
            else:
                before = peak[at, :] if g == 0 else now
                now = jnp.maximum(before, top)
                factor = jnp.exp2(before - now)
            w = jnp.exp2(s - jnp.concatenate([now] * (size // hd), axis=1)).astype(BF16)
            wv = lax.dot_general(w, kv[pl.ds(start, size), hd:], NN, preferred_element_type=F32)
            if g == 0 and fresh:
                total = wv
            else:
                total = (acc[at, :] if g == 0 else total) * jnp.concatenate([factor, factor], axis=1) + wv
            if g + 1 == len(segments):
                if last:
                    out = total[:, 0:hd] / total[:, hd:]
                    ostage[u + t // tiles, (t % tiles) * toks : (t % tiles + 1) * toks] = out.astype(BF16).reshape(
                        toks, group, hd
                    )
                else:
                    peak[at, :] = now
                    acc[at, :] = total

    span_at = pl.multiple_of(prefix + half * span, span)
    whole(raw.at[pl.ds(span_at, span), both], span_recv).wait()
    span_pass = pltpu.make_async_remote_copy(
        raw.at[pl.ds(prefix, span), both], raw.at[pl.ds(prefix, span), both], span_pass_sent, span_pass_recv,
        device_id=partner, device_id_type=MESH,
    )

    @pl.when(half == 0)
    def _():
        span_pass.start()

    key0 = raw[pl.ds(span_at, 16), 0:hd].astype(F32)[0:1, :]
    settle(span_at, span, key0)
    own_rows = slice(0, 2 * part_rows)
    acc[own_rows, :] = jnp.zeros((2 * part_rows, 2 * hd), F32)
    peak[own_rows, :] = jnp.full((2 * part_rows, hd), -1e30, F32)
    for h in range(2):
        whole(qbuf.at[h], q_recv.at[h]).wait()

    def chunk(i, _):
        c = lax.rem(col + (1 - lax.div(i, 3)) * i * (heads - 1) * (1 - lax.div(i, 2)) + lax.div(i, 2) * (i - 1), heads)
        start = pl.multiple_of((half * heads + c) * per_slot, per_slot)
        here = raw.at[pl.ds(start, per_slot), both]
        whole(here, page_recv.at[c]).wait()
        pltpu.make_async_remote_copy(
            here, here, pass_sent, pass_recv.at[c], device_id=partner, device_id_type=MESH
        ).start()
        settle(start, per_slot, key0)
        attend(0, 2, [(start, per_slot, None)], False, False, None)
        return 0

    lax.fori_loop(0, heads, chunk, 0)
    near_at = pl.multiple_of(half * near, near)
    far_at = pl.multiple_of((1 - half) * near, near)
    cut = near // 2

    def halves_of(at):
        return [(pl.multiple_of(at + i * cut, cut), cut, None) for i in range(2)]

    def first_pass(i, _):
        slot, h = unit_of(i)
        u = slot * 2 + h
        whole(qbuf.at[u], q_recv.at[u]).wait()
        attend(u, 1, halves_of(near_at), True, False, None)
        return 0

    lax.fori_loop(0, units, first_pass, 0)

    for c in range(heads):
        start = pl.multiple_of(far_at + c * per_slot, per_slot)
        whole(raw.at[pl.ds(start, per_slot), both], pass_recv.at[c]).wait()
        settle(start, per_slot, key0)

    @pl.when(half == 1)
    def _():
        span_pass.wait_recv()
        settle(prefix, span, key0)

    def second_pass(j, _):
        own = lax.div(j, units)
        slot, h = unit_of((1 - own) * (units - 1 - j))
        slot = (1 - own) * slot
        h = (1 - own) * h + own * (j - units)
        u = slot * 2 + h
        from_col = lax.rem(col - slot + heads, heads)
        first_token = from_col * tokens + h * part
        for z in range(halves):

            @pl.when(half == z)
            def _():
                spans = [(prefix + i * span, span, None) for i in range(z)]
                for w in range(2):

                    @pl.when(lax.div(from_col, heads // 2) == w)
                    def _():
                        last_keys = (prefix + z * span, (w + 1) * span // 2, 0)
                        attend(u, 1, halves_of(far_at) + spans + [last_keys], False, True, first_token)

        o_dst = out_hbm.at[pl.ds(pl.multiple_of(h * part, part), part), pl.ds(pl.multiple_of(col * group, group), group), :]

        @pl.when(own == 1)
        def _():
            pltpu.make_async_copy(ostage.at[u], o_dst, own_sem).start()

        @pl.when(own == 0)
        def _():
            pltpu.make_async_remote_copy(
                ostage.at[u], o_dst, o_sent, o_recv,
                device_id=(me_req, half * heads + from_col), device_id_type=MESH,
            ).start()

        return 0

    lax.fori_loop(0, 2 * heads, second_pass, 0)
    whole(ostage.at[pl.ds(0, 2)], own_sem).wait()
    whole(raw.at[pl.ds(0, (heads - 1) * tokens), both], span_sent).wait()
    whole(raw.at[pl.ds(0, (n_req * heads - 1) * page_len), both], page_sent).wait()
    whole(raw.at[pl.ds(0, near), both], pass_sent).wait()

    @pl.when(half == 0)
    def _():
        span_pass.wait_send()

    whole(qbuf.at[pl.ds(0, units)], q_sent).wait()
    whole(ostage.at[pl.ds(0, units)], o_sent).wait()
    whole(ostage.at[pl.ds(0, units)], o_recv).wait()


def per_device(queries, span_keys, span_values, store_keys, store_values, page_home, hits, counts):
    n_req = lax.axis_size("req")
    n_ctx = lax.axis_size("ctx")
    _, tokens, q_heads, hd = queries.shape
    heads = span_keys.shape[2]
    group = q_heads // heads
    _, store_dev, page_len, _, _ = store_keys.shape
    dims = (n_req, n_ctx, heads, store_dev, page_len, tokens, group, hd)
    rows = heads * tokens * group
    keys = n_req * n_ctx * page_len + n_ctx * tokens
    smem = pl.BlockSpec(memory_space=pltpu.SMEM)
    hbm = pl.BlockSpec(memory_space=pl.ANY)
    dma = pltpu.SemaphoreType.DMA
    out = pl.pallas_call(
        functools.partial(kernel, dims),
        out_shape=jax.ShapeDtypeStruct((tokens, q_heads, hd), BF16),
        in_specs=[smem] * 3 + [hbm] * 5,
        out_specs=hbm,
        scratch_shapes=[
            pltpu.VMEM((2, store_dev, page_len * heads, hd), BF16),
            pltpu.VMEM((2, tokens * heads, hd), BF16),
            pltpu.VMEM((n_req, heads, page_len, 2 * hd), BF16),
            pltpu.VMEM((heads, tokens, 2 * hd), BF16),
            pltpu.VMEM((2 * heads, tokens // 2, group, hd), BF16),
            pltpu.VMEM((keys, 2 * hd), BF16),
            pltpu.VMEM((keys, 3 * hd), BF16),
            pltpu.VMEM((rows, 2 * hd), F32),
            pltpu.VMEM((rows, hd), F32),
            pltpu.VMEM((2 * heads, tokens // 2, group, hd), BF16),
            dma((4,)),
            dma, dma((heads,)), dma, dma, dma, dma((heads,)), dma, dma, dma, dma((2 * heads,)), dma, dma, dma,
        ],
        compiler_params=pltpu.CompilerParams(
            collective_id=0, has_side_effects=True, vmem_limit_bytes=60 * 2**20
        ),
        name="attend_pages",
    )(
        hits, counts, page_home, queries[0],
        span_keys.reshape(tokens * heads, hd),
        span_values.reshape(tokens * heads, hd),
        store_keys.reshape(store_dev, page_len * heads, hd),
        store_values.reshape(store_dev, page_len * heads, hd),
    )
    return out[None]


def solution(mesh):
    placed = (
        P("req", "ctx", None, None),
        P("req", "ctx", None, None),
        P("req", "ctx", None, None),
        P("ctx", "req", None, None, None),
        P("ctx", "req", None, None, None),
        P("ctx", None),
        P(),
        P(),
    )
    return jax.shard_map(
        per_device,
        mesh=mesh,
        in_specs=placed,
        out_specs=P("req", "ctx", None, None),
        check_vma=False,
    )
```

```python
import functools

import jax
import jax.numpy as jnp
from jax import lax
from jax.experimental import pallas as pl
from jax.experimental.pallas import tpu as pltpu
from jax.sharding import PartitionSpec as P

MESH = pl.DeviceIdType.MESH
F32 = jnp.float32
BF16 = jnp.bfloat16
NT = (((1,), (1,)), ((), ()))
NN = (((1,), (0,)), ((), ()))
DEAD = 448.0
LOG2E = 1.4426950408889634
ROWS = 256


def kernel(
    dims, hits, counts, home, q_hbm, sk_hbm, sv_hbm, stk_hbm, stv_hbm, out_hbm,
    store, span_in, send, span_send, qbuf, raw, kv, acc, peak, ostage,
    load_sem, page_sent, page_recv, span_sent, span_recv, pass_sent, pass_recv,
    span_pass_sent, span_pass_recv, q_sent, q_recv, o_sent, o_recv, own_sem,
):
    n_req, n_ctx, heads, store_dev, page_len, tokens, group, hd = dims
    halves = n_ctx // heads
    part = tokens // 2
    piece = page_len * heads
    per_slot = n_req * page_len
    near = heads * per_slot
    prefix = halves * near
    span = heads * tokens
    me_req = lax.axis_index("req")
    me_ctx = lax.axis_index("ctx")
    col = lax.rem(me_ctx, heads)
    half = lax.div(me_ctx, heads)
    partner = (me_req, (1 - half) * heads + col)
    scale = hd ** -0.5 * LOG2E
    both = pl.ds(0, 2 * hd)

    loads = [
        pltpu.make_async_copy(src, dst, load_sem.at[i])
        for i, (src, dst) in enumerate(
            [(sk_hbm, span_in.at[0]), (sv_hbm, span_in.at[1]), (stk_hbm, store.at[0]), (stv_hbm, store.at[1])]
        )
    ]
    for load in loads:
        load.start()

    def whole(ref, sem):
        return pltpu.make_async_copy(ref, ref, sem)

    def q_src(c, h):
        return q_hbm.at[pl.ds(h * part, part), pl.ds(pl.multiple_of(c * group, group), group), :]

    for h in range(2):
        pltpu.make_async_copy(q_src(col, h), qbuf.at[h], q_recv.at[h]).start()

    barrier = pltpu.get_barrier_semaphore()

    def near_device(o):
        req = lax.rem(me_req + lax.div(o, heads), n_req)
        return req, half * heads + lax.rem(col + lax.rem(o, heads), heads)

    def greet(o, _):
        pl.semaphore_signal(barrier, inc=1, device_id=near_device(o), device_id_type=MESH)
        return 0

    lax.fori_loop(1, n_req * heads, greet, 0)
    pl.semaphore_signal(barrier, inc=1, device_id=partner, device_id_type=MESH)

    to = lax.broadcasted_iota(jnp.int32, (piece, piece), 0)
    frm = lax.broadcasted_iota(jnp.int32, (piece, piece), 1)
    swap = (lax.rem(to, page_len) * heads + lax.div(to, page_len) == frm).astype(F32).astype(BF16)

    for load in loads[:2]:
        load.wait()
    for g in range(tokens // page_len):
        pair = jnp.concatenate(
            [span_in[0, g * piece : (g + 1) * piece, :], span_in[1, g * piece : (g + 1) * piece, :]], axis=1
        )
        moved = lax.dot_general(swap, pair, NN, preferred_element_type=F32).astype(BF16)
        for h in range(heads):
            span_send[h, g * page_len : (g + 1) * page_len, :] = moved[h * page_len : (h + 1) * page_len, :]
    for load in loads[2:]:
        load.wait()

    first_row = me_req * store_dev
    group_of = 4

    def pack(r):
        slot = jnp.int32(0)
        live = jnp.int32(0)
        for i in range(n_req):
            j = i * n_ctx + me_ctx
            row = home[0, hits[r, j]] - first_row
            mine = jnp.logical_and(row >= 0, row < store_dev).astype(jnp.int32)
            slot = slot + mine * row
            live = live + mine * (j < counts[r]).astype(jnp.int32)
        live = live.astype(F32)
        pair = jnp.concatenate([store[0, slot], store[1, slot]], axis=1)
        moved = lax.dot_general(swap, pair, NN, preferred_element_type=F32)
        lane = lax.broadcasted_iota(jnp.int32, moved.shape, 1)
        filler = jnp.where(lane < hd, DEAD, 0.0)
        moved = (moved * live + filler * (1.0 - live)).astype(BF16)
        for h in range(heads):
            send[r, h] = moved[h * page_len : (h + 1) * page_len, :]

    def pack_group(i, _):
        for k in range(group_of):
            pack(i * group_of + k)
        return 0

    lax.fori_loop(0, n_req // group_of, pack_group, 0)
    pl.semaphore_wait(barrier, n_req * heads)

    span_dst = raw.at[pl.ds(pl.multiple_of(prefix + me_ctx * tokens, tokens), tokens), both]
    pltpu.make_async_copy(span_send.at[col], span_dst, span_recv).start()

    def send_span(o, _):
        c = lax.rem(col + o, heads)
        pltpu.make_async_remote_copy(
            span_send.at[c], span_dst, span_sent, span_recv,
            device_id=(me_req, half * heads + c), device_id_type=MESH,
        ).start()
        return 0

    lax.fori_loop(1, heads, send_span, 0)

    page_dst = raw.at[pl.ds(pl.multiple_of((me_ctx * n_req + me_req) * page_len, page_len), page_len), both]
    pltpu.make_async_copy(send.at[me_req, col], page_dst, page_recv.at[col]).start()

    def send_page(req, c):
        pltpu.make_async_remote_copy(
            send.at[req, c], page_dst, page_sent, page_recv.at[col],
            device_id=(req, half * heads + c), device_id_type=MESH,
        ).start()

    def mixed(o):
        return lax.rem(me_req + 5 * o, n_req)

    def send_same(o, _):
        send_page(mixed(o), col)
        return 0

    lax.fori_loop(1, n_req, send_same, 0)

    def send_sides(o, _):
        req = mixed(o)
        send_page(req, lax.rem(col + 1, heads))
        send_page(req, lax.rem(col + heads - 1, heads))
        return 0

    lax.fori_loop(0, n_req, send_sides, 0)

    def send_far(o, _):
        send_page(mixed(o), lax.rem(col + 2, heads))
        return 0

    lax.fori_loop(0, n_req, send_far, 0)

    def unit_of(i):
        far = lax.div(i, 4)
        slot = (1 - far) * (1 + 2 * lax.rem(i, 2)) + far * 2
        return slot, (1 - far) * lax.div(i, 2) + far * (i - 4)

    def send_q(i, _):
        slot, h = unit_of(i)
        c = lax.rem(col + slot, heads)
        u = slot * 2 + h
        pltpu.make_async_remote_copy(
            q_src(c, h), qbuf.at[u], q_sent, q_recv.at[u],
            device_id=(me_req, half * heads + c), device_id_type=MESH,
        ).start()
        return 0

    units = 2 * (heads - 1)
    lax.fori_loop(0, units, send_q, 0)

    def settle(start, size, key0):
        at = pl.ds(start, size)
        keys = raw[at, 0:hd].astype(F32)
        dead = keys > 100.0
        kv[at, 0:hd] = jnp.where(dead, key0, keys).astype(BF16)
        kv[at, hd : 2 * hd] = raw[at, hd : 2 * hd]
        kv[at, 2 * hd :] = jnp.where(dead, 0.0, 1.0).astype(BF16)

    part_rows = part * group
    tiles = part_rows // ROWS
    toks = ROWS // group

    def attend(u, count, segments, fresh, last, first_token):
        base = u * part_rows
        steps = [(t, g) for t in range(count * tiles) for g in range(len(segments))]

        def score(t, g):
            start, size, _ = segments[g]
            q = qbuf[u + t // tiles, (t % tiles) * toks : (t % tiles + 1) * toks].reshape(ROWS, hd)
            return lax.dot_general(q, kv[pl.ds(start, size), 0:hd], NT, preferred_element_type=F32)

        following = score(*steps[0])
        for n, (t, g) in enumerate(steps):
            s = following * scale
            if n + 1 < len(steps):
                following = score(*steps[n + 1])
            start, size, first_key = segments[g]
            at = pl.ds(pl.multiple_of(base + t * ROWS, ROWS), ROWS)
            if first_key is not None:
                token = lax.broadcasted_iota(jnp.int32, (ROWS, size), 0) // group + (first_token + t * toks - first_key)
                key = lax.broadcasted_iota(jnp.int32, (ROWS, size), 1)
                s = jnp.where(key <= token, s, -1e30)
            top = jnp.max(s, axis=1, keepdims=True)
            if g == 0 and fresh:
                now = jnp.broadcast_to(top, (ROWS, hd))
            else:
                before = peak[at, :] if g == 0 else now
                now = jnp.maximum(before, top)
                factor = jnp.exp2(before - now)
            w = jnp.exp2(s - jnp.concatenate([now] * (size // hd), axis=1)).astype(BF16)
            wv = lax.dot_general(w, kv[pl.ds(start, size), hd:], NN, preferred_element_type=F32)
            if g == 0 and fresh:
                total = wv
            else:
                total = (acc[at, :] if g == 0 else total) * jnp.concatenate([factor, factor], axis=1) + wv
            if g + 1 == len(segments):
                if last:
                    out = total[:, 0:hd] / total[:, hd:]
                    ostage[u + t // tiles, (t % tiles) * toks : (t % tiles + 1) * toks] = out.astype(BF16).reshape(
                        toks, group, hd
                    )
                else:
                    peak[at, :] = now
                    acc[at, :] = total

    span_at = pl.multiple_of(prefix + half * span, span)
    whole(raw.at[pl.ds(span_at, span), both], span_recv).wait()
    span_pass = pltpu.make_async_remote_copy(
        raw.at[pl.ds(prefix, span), both], raw.at[pl.ds(prefix, span), both], span_pass_sent, span_pass_recv,
        device_id=partner, device_id_type=MESH,
    )

    @pl.when(half == 0)
    def _():
        span_pass.start()

    key0 = raw[pl.ds(span_at, 16), 0:hd].astype(F32)[0:1, :]
    settle(span_at, span, key0)
    own_rows = slice(0, 2 * part_rows)
    acc[own_rows, :] = jnp.zeros((2 * part_rows, 2 * hd), F32)
    peak[own_rows, :] = jnp.full((2 * part_rows, hd), -1e30, F32)
    for h in range(2):
        whole(qbuf.at[h], q_recv.at[h]).wait()

    def chunk(i, _):
        c = lax.rem(col + (1 - lax.div(i, 3)) * i * (heads - 1) * (1 - lax.div(i, 2)) + lax.div(i, 2) * (i - 1), heads)
        start = pl.multiple_of((half * heads + c) * per_slot, per_slot)
        here = raw.at[pl.ds(start, per_slot), both]
        whole(here, page_recv.at[c]).wait()
        pltpu.make_async_remote_copy(
            here, here, pass_sent, pass_recv.at[c], device_id=partner, device_id_type=MESH
        ).start()
        settle(start, per_slot, key0)
        attend(0, 2, [(start, per_slot, None)], False, False, None)
        return 0

    lax.fori_loop(0, heads, chunk, 0)
    near_at = pl.multiple_of(half * near, near)
    far_at = pl.multiple_of((1 - half) * near, near)
    cut = near // 2

    def halves_of(at):
        return [(pl.multiple_of(at + i * cut, cut), cut, None) for i in range(2)]

    def first_pass(i, _):
        slot, h = unit_of(i)
        u = slot * 2 + h
        whole(qbuf.at[u], q_recv.at[u]).wait()
        attend(u, 1, halves_of(near_at), True, False, None)
        return 0

    lax.fori_loop(0, units, first_pass, 0)

    for c in range(heads):
        start = pl.multiple_of(far_at + c * per_slot, per_slot)
        whole(raw.at[pl.ds(start, per_slot), both], pass_recv.at[c]).wait()
        settle(start, per_slot, key0)

    @pl.when(half == 1)
    def _():
        span_pass.wait_recv()
        settle(prefix, span, key0)

    def second_pass(j, _):
        own = lax.div(j, units)
        slot, h = unit_of((1 - own) * (units - 1 - j))
        slot = (1 - own) * slot
        h = (1 - own) * h + own * (j - units)
        u = slot * 2 + h
        from_col = lax.rem(col - slot + heads, heads)
        first_token = from_col * tokens + h * part
        for z in range(halves):

            @pl.when(half == z)
            def _():
                spans = [(prefix + i * span, span, None) for i in range(z)]
                for w in range(2):

                    @pl.when(lax.div(from_col, heads // 2) == w)
                    def _():
                        last_keys = (prefix + z * span, (w + 1) * span // 2, 0)
                        attend(u, 1, halves_of(far_at) + spans + [last_keys], False, True, first_token)

        o_dst = out_hbm.at[pl.ds(pl.multiple_of(h * part, part), part), pl.ds(pl.multiple_of(col * group, group), group), :]

        @pl.when(own == 1)
        def _():
            pltpu.make_async_copy(ostage.at[u], o_dst, own_sem).start()

        @pl.when(own == 0)
        def _():
            pltpu.make_async_remote_copy(
                ostage.at[u], o_dst, o_sent, o_recv,
                device_id=(me_req, half * heads + from_col), device_id_type=MESH,
            ).start()

        return 0

    lax.fori_loop(0, 2 * heads, second_pass, 0)
    whole(ostage.at[pl.ds(0, 2)], own_sem).wait()
    whole(raw.at[pl.ds(0, (heads - 1) * tokens), both], span_sent).wait()
    whole(raw.at[pl.ds(0, (n_req * heads - 1) * page_len), both], page_sent).wait()
    whole(raw.at[pl.ds(0, near), both], pass_sent).wait()

    @pl.when(half == 0)
    def _():
        span_pass.wait_send()

    whole(qbuf.at[pl.ds(0, units)], q_sent).wait()
    whole(ostage.at[pl.ds(0, units)], o_sent).wait()
    whole(ostage.at[pl.ds(0, units)], o_recv).wait()


def per_device(queries, span_keys, span_values, store_keys, store_values, page_home, hits, counts):
    n_req = lax.axis_size("req")
    n_ctx = lax.axis_size("ctx")
    _, tokens, q_heads, hd = queries.shape
    heads = span_keys.shape[2]
    group = q_heads // heads
    _, store_dev, page_len, _, _ = store_keys.shape
    dims = (n_req, n_ctx, heads, store_dev, page_len, tokens, group, hd)
    rows = heads * tokens * group
    keys = n_req * n_ctx * page_len + n_ctx * tokens
    smem = pl.BlockSpec(memory_space=pltpu.SMEM)
    hbm = pl.BlockSpec(memory_space=pl.ANY)
    dma = pltpu.SemaphoreType.DMA
    out = pl.pallas_call(
        functools.partial(kernel, dims),
        out_shape=jax.ShapeDtypeStruct((tokens, q_heads, hd), BF16),
        in_specs=[smem] * 3 + [hbm] * 5,
        out_specs=hbm,
        scratch_shapes=[
            pltpu.VMEM((2, store_dev, page_len * heads, hd), BF16),
            pltpu.VMEM((2, tokens * heads, hd), BF16),
            pltpu.VMEM((n_req, heads, page_len, 2 * hd), BF16),
            pltpu.VMEM((heads, tokens, 2 * hd), BF16),
            pltpu.VMEM((2 * heads, tokens // 2, group, hd), BF16),
            pltpu.VMEM((keys, 2 * hd), BF16),
            pltpu.VMEM((keys, 3 * hd), BF16),
            pltpu.VMEM((rows, 2 * hd), F32),
            pltpu.VMEM((rows, hd), F32),
            pltpu.VMEM((2 * heads, tokens // 2, group, hd), BF16),
            dma((4,)),
            dma, dma((heads,)), dma, dma, dma, dma((heads,)), dma, dma, dma, dma((2 * heads,)), dma, dma, dma,
        ],
        compiler_params=pltpu.CompilerParams(
            collective_id=0, has_side_effects=True, vmem_limit_bytes=60 * 2**20
        ),
        name="attend_pages",
    )(
        hits, counts, page_home, queries[0],
        span_keys.reshape(tokens * heads, hd),
        span_values.reshape(tokens * heads, hd),
        store_keys.reshape(store_dev, page_len * heads, hd),
        store_values.reshape(store_dev, page_len * heads, hd),
    )
    pieces = 4

    def hand_over(src, dst, held, arrived, left):
        size = tokens // pieces
        at = [pl.ds(i * size, size) for i in range(pieces)]
        gets = [pltpu.make_async_copy(src.at[at[i]], held.at[at[i]], arrived.at[i]) for i in range(pieces)]
        puts = [pltpu.make_async_copy(held.at[at[i]], dst.at[at[i]], left.at[i]) for i in range(pieces)]
        for get in gets:
            get.start()
        for get, put in zip(gets, puts):
            get.wait()
            put.start()
        for put in puts:
            put.wait()

    out = pl.pallas_call(
        hand_over,
        out_shape=jax.ShapeDtypeStruct(out.shape, out.dtype),
        in_specs=[hbm],
        out_specs=hbm,
        scratch_shapes=[pltpu.VMEM(out.shape, out.dtype), dma((pieces,)), dma((pieces,))],
        compiler_params=pltpu.CompilerParams(vmem_limit_bytes=60 * 2**20),
        name="hand_over",
    )(out)
    return out[None]


def solution(mesh):
    placed = (
        P("req", "ctx", None, None),
        P("req", "ctx", None, None),
        P("req", "ctx", None, None),
        P("ctx", "req", None, None, None),
        P("ctx", "req", None, None, None),
        P("ctx", None),
        P(),
        P(),
    )
    return jax.shard_map(
        per_device,
        mesh=mesh,
        in_specs=placed,
        out_specs=P("req", "ctx", None, None),
        check_vma=False,
    )
```
